32 devices in a mesh: row: 4 (over y, x), col: 8 (over z, core).
Axes of the slice: x: 2, y: 2, z: 4, core: 2. Of those that a mesh axis runs over, the one named last changes fastest.
Arguments:
- left_factor: float32 [2048, 512], P(('row', 'col')), may hold values from -0.125 to 0.125
- left_cotangent: float32 [2048, 512], P(('row', 'col')), may hold values from -32 to 32
- right_factor: float32 [6144, 512], P(('col', 'row')), may hold values from -0.078125 to 0.078125
- right_cotangent: float32 [6144, 512], P(('col', 'row')), may hold values from -32 to 32
- singular: float32 [512], replicated, may hold values from 0.5 to 2, as said below
- singular_cotangent: float32 [512], replicated, may hold values from -384 to 384
Outputs:
- matrix_cotangent: float32 [2048, 6144], P('row', 'col')
The draws below stay inside these ranges and needn't reach their ends.
Inputs may be any that keep to these rules, and one draw needn't show every extreme that they name: `singular`: strictly decreasing; consecutive values differ by at least 0.75 / 512.
All inputs are finite; a program needn't handle non-finite values.
Results may differ from the reference program's by a relative error of at most 0.0003.
Values sent between devices are 32-bit elements; how exact they have to be, the bound alone decides.
A program may use at most 64 MiB of HBM per device.

```python
import jax
import jax.numpy as jnp
from jax import lax

K = 512
M = 2048
N = 6144


def draw_singular(key, part):
    jitter = jax.random.uniform(jax.random.fold_in(key, 7), (K,), jnp.float32, 0.0, 0.5)
    steps = jnp.arange(K).astype(jnp.float32)
    return (2.0 - 1.5 * (steps + jitter) / K).astype(jnp.float32)


def spiked(values, own_key, source, target, blocks, factor):
    owner, partner = [(jnp.arange(values.shape[dim]) // (values.shape[dim] // blocks)).reshape([-1 if axis == dim else 1 for axis in range(values.ndim)]) for dim in (source, target)]
    chosen = jax.random.permutation(own_key, blocks)[partner]
    strong = (owner == chosen) | (owner == (partner + blocks // 2) % blocks)
    return jnp.where(strong, factor * values, values)


def block_levels(own_key, shape, shards, least, top_value):
    def one(position, parts):
        heights = jax.random.uniform(jax.random.fold_in(jax.random.fold_in(own_key, 6), position), (parts,), jnp.float32, least / len(shards), top_value / len(shards))
        return jnp.repeat(jnp.exp(heights), shape[position] // parts).reshape((-1,) + (1,) * (len(shape) - position - 1))

    factor_of = one(*shards[0])
    for cut in shards[1:]:
        factor_of = factor_of * one(*cut)
    return factor_of


def scatter_about(own_key, shape, scale, reach, split=(), kind=jnp.bfloat16):
    entries = jax.random.normal(own_key, shape, jnp.float32) * scale
    if len(split) > 0:
        entries = block_levels(own_key, shape, split, -0.22, 0.18) * entries
    return jnp.clip(entries, min=-reach, max=reach).astype(kind)


def gaussian_with(stream_key, extent, deviation, most, split, heavy, held_as=jnp.bfloat16):
    drawn = deviation * jax.random.normal(stream_key, extent, jnp.float32)
    if split:
        drawn = drawn * block_levels(stream_key, extent, split, -0.22, 0.18)
    return jnp.clip(spiked(drawn, jax.random.fold_in(stream_key, 3), *heavy), -most, most).astype(held_as)


def setup_inputs(seed: int = 0) -> dict:
    key_list = jax.random.split(jax.random.key(seed), 7)
    return {
        "left_factor": scatter_about(key_list[0], (M, K), M ** -0.5, 0.125, ((0, 32),), jnp.float32),
        "left_cotangent": gaussian_with(key_list[1], (M, K), 3.0, 32.0, ((0, 32),), (0, 1, 32, 2.75), jnp.float32),
        "right_factor": scatter_about(key_list[2], (N, K), N ** -0.5, 0.078125, ((0, 32),), jnp.float32),
        "right_cotangent": gaussian_with(key_list[3], (N, K), 3.0, 32.0, ((0, 32),), (0, 1, 32, 2.75), jnp.float32),
        "singular": draw_singular(jax.random.fold_in(key_list[6], 71), 0),
        "singular_cotangent": scatter_about(key_list[5], (K,), 64.0, 384.0, (), jnp.float32),
    }


def reference(left_factor, left_cotangent, right_factor, right_cotangent, singular, singular_cotangent):
    highest = lax.Precision.HIGHEST
    gram_left = jnp.dot(left_factor.T, left_cotangent, precision=highest, preferred_element_type=jnp.float32)
    gram_right = jnp.dot(right_factor.T, right_cotangent, precision=highest, preferred_element_type=jnp.float32)
    squares = singular * singular
    spread = squares[None, :] - squares[:, None]
    diagonal = jnp.eye(K, dtype=jnp.bool_)
    divided = jnp.where(diagonal, jnp.float32(0.0), 1.0 / jnp.where(diagonal, jnp.float32(1.0), spread))
    inverse = 1.0 / singular
    core = (divided * (gram_left - gram_left.T)) * singular[None, :]
    core = core + jnp.diag(singular_cotangent)
    core = core + singular[:, None] * (divided * (gram_right - gram_right.T))
    core = core - gram_left * inverse[None, :] - inverse[:, None] * gram_right.T
    left_panel = jnp.dot(left_factor, core, precision=highest, preferred_element_type=jnp.float32) + left_cotangent * inverse[None, :]
    scaled_right = right_cotangent * inverse[None, :]
    dims = (((1,), (1,)), ((), ()))
    result = lax.dot_general(left_panel, right_factor, dims, precision=highest, preferred_element_type=jnp.float32)
    result = result + lax.dot_general(left_factor, scaled_right, dims, precision=highest, preferred_element_type=jnp.float32)
    return result
```

```python
import functools
import math

import jax
import jax.numpy as jnp
from jax import lax
from jax.experimental import pallas as pl
from jax.experimental.pallas import tpu as pltpu
from jax.sharding import PartitionSpec as P

MESH = pl.DeviceIdType.MESH
F32 = jnp.float32
BF16 = jnp.bfloat16
LANES = 128
NT = (((1,), (1,)), ((), ()))
NN = (((1,), (0,)), ((), ()))
TN = (((0,), (0,)), ((), ()))


def split(x):
    hi = x.astype(BF16)
    return hi, (x - hi.astype(F32)).astype(BF16)


def dot3(ah, al, bh, bl, dims):
    dot = functools.partial(lax.dot_general, dimension_numbers=dims, preferred_element_type=F32)
    return dot(ah, bh) + (dot(ah, bl) + dot(al, bh))


def kernel(
    R, C,
    u_ref, uc_ref, v_ref, vc_ref, s_ref, sc_ref, out_ref,
    ug, ucg, vg, vcg, gl, gr, scol, part, ra, p1, rb, rc, core,
    wh, wl, uh, ul, lh, ll, xh, xl,
    send_v, send_u, send_r, send_c, recv_v, recv_u, recv_a, recv_b, recv_c, recv_d, recv_e,
):
    n = math.isqrt(R)
    Z = C // 2
    r, c = lax.axis_index("row"), lax.axis_index("col")
    a, b = r // n, r % n
    z, h = c // 2, c % 2
    sib = (r, c + 1 - 2 * h)
    um, vm = u_ref.shape[0], v_ref.shape[0]
    K = u_ref.shape[1]
    half = K // 2
    blk = half // R

    def row_peer(k):
        return lax.rem(r + k, R)

    def z_peer(k):
        return lax.rem(z + k, Z)

    def a_peer(k):
        return lax.rem(a + k, n)

    def b_peer(k):
        return lax.rem(b + k, n)

    barrier = pltpu.get_barrier_semaphore()
    pl.semaphore_signal(barrier, inc=1, device_id=sib, device_id_type=MESH)
    for k in range(1, R):
        pl.semaphore_signal(barrier, inc=1, device_id=(row_peer(k), c), device_id_type=MESH)
    for k in range(1, Z):
        pl.semaphore_signal(barrier, inc=1, device_id=(r, 2 * z_peer(k) + h), device_id_type=MESH)
    pl.semaphore_wait(barrier, 1 + (R - 1) + (Z - 1))

    sends = []
    counts = {"v": 0, "u": 0, "r": 0, "c": 0}
    pools = {"v": send_v, "u": send_u, "r": send_r, "c": send_c}

    def push(pool, src, dst, recv, to):
        i = counts[pool]
        counts[pool] = i + 1
        copy = pltpu.make_async_remote_copy(
            src_ref=src, dst_ref=dst, send_sem=pools[pool].at[i], recv_sem=recv,
            device_id=to, device_id_type=MESH,
        )
        copy.start()
        sends.append(copy)

    def await_recv(dst, recv):
        pltpu.make_async_remote_copy(
            src_ref=dst, dst_ref=dst, send_sem=send_v.at[0], recv_sem=recv,
            device_id=sib, device_id_type=MESH,
        ).wait_recv()

    def rows(ref, index, size):
        return ref.at[pl.ds(pl.multiple_of(index * size, size), size)]

    vbuf, ubuf = (vg, vcg), (ug, ucg)
    vsrc, usrc = (v_ref, vc_ref), (u_ref, uc_ref)

    for k in range(1, n):
        push("v", v_ref, rows(vg, r, vm), recv_v.at[0, r], (a * n + b_peer(k), c))
    for k in range(1, n):
        push("v", vc_ref, rows(vcg, r, vm), recv_v.at[1, r], (a_peer(k) * n + b, c))
    for t in range(2):
        for k in range(1, Z):
            push("u", usrc[t], rows(ubuf[t], c, um), recv_u.at[t, c], (r, 2 * z_peer(k) + h))
    for k in range(1, n):
        push("v", v_ref, rows(vg, r, vm), recv_v.at[0, r], (a_peer(k) * n + b, c))
    for k in range(1, n):
        push("v", vc_ref, rows(vcg, r, vm), recv_v.at[1, r], (a * n + b_peer(k), c))
    for t in range(2):
        push("c", usrc[t], rows(ubuf[t], c, um), recv_u.at[t, c], sib)

    highest = lax.Precision.HIGHEST
    gl[...] = lax.dot_general(u_ref[...], uc_ref[...], TN, precision=highest, preferred_element_type=F32)
    gr[...] = lax.dot_general(v_ref[...], vc_ref[...], TN, precision=highest, preferred_element_type=F32)
    s_row = s_ref[...]
    inv_row = 1.0 / s_row
    scol[...] = jnp.broadcast_to(s_row, (LANES, K)).T

    @pl.loop(0, K // LANES)
    def _(i):
        here = pl.ds(pl.multiple_of(i * LANES, LANES), LANES)
        s_col = scol[here, 0:1]
        inv_col = 1.0 / s_col
        spread = s_row * s_row - s_col * s_col
        row_id = i * LANES + lax.broadcasted_iota(jnp.int32, (LANES, K), 0)
        diagonal = row_id == lax.broadcasted_iota(jnp.int32, (LANES, K), 1)
        divided = jnp.where(diagonal, 0.0, 1.0 / jnp.where(diagonal, 1.0, spread))
        left, left_t = gl[here, :], gl[:, here].T
        right, right_t = gr[here, :], gr[:, here].T
        value = divided * (left - left_t) * s_row + s_col * (divided * (right - right_t))
        part[here, :] = value - left * inv_row - inv_col * right_t

    push("c", rows(part, 1 - h, half), ra, recv_a.at[0], sib)
    rows(ug, c, um)[...] = u_ref[...]
    rows(ucg, c, um)[...] = uc_ref[...]
    rows(vg, r, vm)[...] = v_ref[...]
    rows(vcg, r, vm)[...] = vc_ref[...]
    await_recv(ra, recv_a.at[0])
    p1[...] = rows(part, h, half)[...] + ra[...]
    for k in range(1, R):
        push("r", rows(p1, row_peer(k), blk), rows(rb, r, blk), recv_b.at[r], (row_peer(k), c))
    rows(rb, r, blk)[...] = rows(p1, r, blk)[...]
    for k in range(1, R):
        await_recv(rows(rb, row_peer(k), blk), recv_b.at[row_peer(k)])
    total = rb[0:blk, :]
    for q in range(1, R):
        total = total + rb[q * blk:(q + 1) * blk, :]
    rows(rc, z, blk)[...] = total
    for k in range(1, Z):
        push("r", rows(rc, z, blk), rows(rc, z, blk), recv_c.at[z], (r, 2 * z_peer(k) + h))

    for k in range(1, n):
        src = a * n + b_peer(k)
        await_recv(rows(vg, src, vm), recv_v.at[0, src])
        for j in range(1, n):
            push("v", rows(vg, src, vm), rows(vg, src, vm), recv_v.at[0, src], (a_peer(j) * n + b, c))
    for k in range(1, n):
        src = a_peer(k) * n + b
        await_recv(rows(vcg, src, vm), recv_v.at[1, src])
        for j in range(1, n):
            push("v", rows(vcg, src, vm), rows(vcg, src, vm), recv_v.at[1, src], (a * n + b_peer(j), c))

    for k in range(1, Z):
        await_recv(rows(rc, z_peer(k), blk), recv_c.at[z_peer(k)])
    total = rc[0:blk, :]
    for q in range(1, Z):
        total = total + rc[q * blk:(q + 1) * blk, :]
    mine = h * R + r
    row_id = mine * blk + lax.broadcasted_iota(jnp.int32, (blk, K), 0)
    diagonal = row_id == lax.broadcasted_iota(jnp.int32, (blk, K), 1)
    rows(core, mine, blk)[...] = total + jnp.where(diagonal, sc_ref[...], 0.0)
    for k in range(1, R):
        push("r", rows(core, mine, blk), rows(core, mine, blk), recv_d.at[r], (row_peer(k), c))
    push("c", rows(core, mine, blk), rows(core, mine, blk), recv_e.at[r], sib)

    for k in range(1, Z):
        src = 2 * z_peer(k) + h
        for t in range(2):
            await_recv(rows(ubuf[t], src, um), recv_u.at[t, src])
            push("c", rows(ubuf[t], src, um), rows(ubuf[t], src, um), recv_u.at[t, src], sib)

    for k in range(1, R):
        q = row_peer(k)
        await_recv(rows(core, h * R + q, blk), recv_d.at[q])
        push("c", rows(core, h * R + q, blk), rows(core, h * R + q, blk), recv_e.at[q], sib)
    for k in range(Z):
        src = 2 * z_peer(k) + 1 - h
        for t in range(2):
            await_recv(rows(ubuf[t], src, um), recv_u.at[t, src])

    uh[...], ul[...] = split(ug[...])
    xh[...], xl[...] = split(ug[...] * inv_row)
    late_a, late_b = [], []
    for k in range(1, n):
        await_recv(rows(vcg, a * n + b_peer(k), vm), recv_v.at[1, a * n + b_peer(k)])
        await_recv(rows(vg, a_peer(k) * n + b, vm), recv_v.at[0, a_peer(k) * n + b])
    for k in range(1, n):
        for j in range(1, n):
            src = a_peer(k) * n + b_peer(j)
            await_recv(rows(vcg, src, vm), recv_v.at[1, src])
            await_recv(rows(vg, src, vm), recv_v.at[0, src])
    width = 2 * LANES

    @pl.loop(0, out_ref.shape[1] // width)
    def _(i):
        here = pl.ds(pl.multiple_of(i * width, width), width)
        bh, bl = split(vcg[here, :])
        out_ref[:, here] = dot3(xh[...], xl[...], bh, bl, NT)

    for q in range(R):
        at = (1 - h) * R + q
        await_recv(rows(core, at, blk), recv_e.at[q])
    wh[...], wl[...] = split(core[...])

    @pl.loop(0, K // width)
    def _(i):
        here = pl.ds(pl.multiple_of(i * width, width), width)
        panel = dot3(uh[...], ul[...], wh[:, here], wl[:, here], NN)
        panel = panel + ucg[:, here] * (1.0 / s_ref[:, here])
        lh[:, here], ll[:, here] = split(panel)

    @pl.loop(0, out_ref.shape[1] // width)
    def _(i):
        here = pl.ds(pl.multiple_of(i * width, width), width)
        bh, bl = split(vg[here, :])
        out_ref[:, here] += dot3(lh[...], ll[...], bh, bl, NT)

    for copy in sends:
        copy.wait_send()


def local(R, C, left_factor, left_cotangent, right_factor, right_cotangent, singular, singular_cotangent):
    um, K = left_factor.shape
    vm = right_factor.shape[0]
    n, Z = math.isqrt(R), C // 2
    M, N = um * C, vm * R
    blk = K // 2 // R
    vmem = pl.BlockSpec(memory_space=pltpu.VMEM)
    dma = pltpu.SemaphoreType.DMA
    f32 = [
        (M, K), (M, K), (N, K), (N, K), (K, K), (K, K), (K, LANES), (K, K),
        (K // 2, K), (K // 2, K), (R * blk, K), (Z * blk, K), (K, K),
    ]
    b16 = [(K, K)] * 2 + [(M, K)] * 6
    scratch = [pltpu.VMEM(shape, F32) for shape in f32] + [pltpu.VMEM(shape, BF16) for shape in b16]
    scratch += [
        dma((4 * (n - 1) + 2 * (n - 1) ** 2,)), dma((2 * (Z - 1),)),
        dma((2 * (R - 1) + Z - 1,)), dma((2 + 1 + 1 + 2 * (Z - 1) + R - 1,)),
        dma((2, R)), dma((2, C)), dma((1,)), dma((R,)), dma((Z,)), dma((R,)), dma((R,)),
    ]
    return pl.pallas_call(
        functools.partial(kernel, R, C),
        out_shape=jax.ShapeDtypeStruct((M, N), F32),
        in_specs=[vmem] * 6,
        out_specs=vmem,
        scratch_shapes=scratch,
        compiler_params=pltpu.CompilerParams(
            collective_id=0, has_side_effects=True, vmem_limit_bytes=48 * 1024 * 1024
        ),
    )(
        left_factor, left_cotangent, right_factor, right_cotangent,
        singular.reshape(1, K), singular_cotangent.reshape(1, K),
    )


def solution(mesh):
    placed = (
        P(("row", "col"), None),
        P(("row", "col"), None),
        P(("col", "row"), None),
        P(("col", "row"), None),
        P(),
        P(),
    )
    return jax.shard_map(
        functools.partial(local, mesh.shape["row"], mesh.shape["col"]),
        mesh=mesh, in_specs=placed, out_specs=P("row", "col"), check_vma=False,
    )
```

```python
import functools
import math

import jax
import jax.numpy as jnp
from jax import lax
from jax.experimental import pallas as pl
from jax.experimental.pallas import tpu as pltpu
from jax.sharding import PartitionSpec as P

MESH = pl.DeviceIdType.MESH
F32 = jnp.float32
BF16 = jnp.bfloat16
LANES = 128
NT = (((1,), (1,)), ((), ()))
NN = (((1,), (0,)), ((), ()))
TN = (((0,), (0,)), ((), ()))


def split(x):
    hi = x.astype(BF16)
    return hi, (x - hi.astype(F32)).astype(BF16)


def dot3(ah, al, bh, bl, dims):
    dot = functools.partial(lax.dot_general, dimension_numbers=dims, preferred_element_type=F32)
    return dot(ah, bh) + (dot(ah, bl) + dot(al, bh))


def kernel(
    R, C,
    u_ref, uc_ref, v_ref, vc_ref, s_ref, sc_ref, out_ref,
    ug, ucg, vg, vcg, gl, gr, scol, part, ra, p1, rb, p2, rc, core,
    wh, wl, uh, ul, lh, ll, xh, xl,
    load, send, recv_v, recv_u, recv_a, recv_b, recv_c, recv_d, recv_e, recv_f,
):
    n = math.isqrt(R)
    Z = C // 2
    r, c = lax.axis_index("row"), lax.axis_index("col")
    a, b = r // n, r % n
    z, h = c // 2, c % 2
    sib = (r, c + 1 - 2 * h)
    um, vm = u_ref.shape[0], v_ref.shape[0]
    K = u_ref.shape[1]
    half = K // 2
    blk = half // R
    piece = blk // Z if blk % (8 * Z) == 0 else blk

    def row_peer(k):
        return lax.rem(r + k, R)

    def z_peer(k):
        return lax.rem(z + k, Z)

    def a_peer(k):
        return lax.rem(a + k, n)

    def b_peer(k):
        return lax.rem(b + k, n)

    def rows(ref, index, size):
        return ref.at[pl.ds(pl.multiple_of(index * size, size), size)]

    loads = [
        pltpu.make_async_copy(src, dst, load.at[i])
        for i, (src, dst) in enumerate((
            (u_ref, rows(ug, c, um)), (uc_ref, rows(ucg, c, um)),
            (v_ref, rows(vg, r, vm)), (vc_ref, rows(vcg, r, vm)),
        ))
    ]
    for copy in loads:
        copy.start()

    barrier = pltpu.get_barrier_semaphore()
    pl.semaphore_signal(barrier, inc=1, device_id=sib, device_id_type=MESH)
    for k in range(1, R):
        pl.semaphore_signal(barrier, inc=1, device_id=(row_peer(k), c), device_id_type=MESH)
    for k in range(1, Z):
        pl.semaphore_signal(barrier, inc=1, device_id=(r, 2 * z_peer(k) + h), device_id_type=MESH)
    pl.semaphore_wait(barrier, 1 + (R - 1) + (Z - 1))

    sends = []

    def push(tag, src, dst, recv, to):
        copy = pltpu.make_async_remote_copy(
            src_ref=src, dst_ref=dst, send_sem=send.at[len(sends)], recv_sem=recv,
            device_id=to, device_id_type=MESH,
        )
        copy.start()
        sends.append(copy)

    def await_recv(tag, dst, recv):
        pltpu.make_async_remote_copy(
            src_ref=dst, dst_ref=dst, send_sem=send.at[0], recv_sem=recv,
            device_id=sib, device_id_type=MESH,
        ).wait_recv()


    for k in range(1, n):
        push("v", v_ref, rows(vg, r, vm), recv_v.at[0, r], (a * n + b_peer(k), c))
    for k in range(1, n):
        push("v", vc_ref, rows(vcg, r, vm), recv_v.at[1, r], (a_peer(k) * n + b, c))
    for k in range(1, Z):
        push("u", u_ref, rows(ug, c, um), recv_u.at[0, c], (r, 2 * z_peer(k) + h))

    highest = lax.Precision.HIGHEST
    for copy in loads:
        copy.wait()
    gl[...] = lax.dot_general(
        rows(ug, c, um)[...], rows(ucg, c, um)[...], TN, precision=highest, preferred_element_type=F32
    )
    gr[...] = lax.dot_general(
        rows(vg, r, vm)[...], rows(vcg, r, vm)[...], TN, precision=highest, preferred_element_type=F32
    )
    s_row = s_ref[...]
    inv_row = 1.0 / s_row
    scol[...] = jnp.broadcast_to(s_row, (LANES, K)).T

    @pl.loop(0, K // LANES)
    def _(i):
        here = pl.ds(pl.multiple_of(i * LANES, LANES), LANES)
        s_col = scol[here, 0:1]
        inv_col = 1.0 / s_col
        spread = s_row * s_row - s_col * s_col
        row_id = i * LANES + lax.broadcasted_iota(jnp.int32, (LANES, K), 0)
        diagonal = row_id == lax.broadcasted_iota(jnp.int32, (LANES, K), 1)
        divided = jnp.where(diagonal, 0.0, 1.0 / jnp.where(diagonal, 1.0, spread))
        left, left_t = gl[here, :], gl[:, here].T
        right, right_t = gr[here, :], gr[:, here].T
        value = divided * (left - left_t) * s_row + s_col * (divided * (right - right_t))
        part[here, :] = value - left * inv_row - inv_col * right_t

    push("a", rows(part, 1 - h, half), ra, recv_a.at[0], sib)
    await_recv("a", ra, recv_a.at[0])
    p1[...] = rows(part, h, half)[...] + ra[...]
    for k in range(1, R):
        push("b", rows(p1, row_peer(k), blk), rows(rb, r, blk), recv_b.at[r], (row_peer(k), c))
    rows(rb, r, blk)[...] = rows(p1, r, blk)[...]
    for k in range(1, n):
        push("v", v_ref, rows(vg, r, vm), recv_v.at[0, r], (a_peer(k) * n + b, c))
    for k in range(1, n):
        push("v", vc_ref, rows(vcg, r, vm), recv_v.at[1, r], (a * n + b_peer(k), c))
    push("w", u_ref, rows(ug, c, um), recv_u.at[0, c], sib)
    push("w", uc_ref, rows(ucg, c, um), recv_u.at[1, c], sib)
    for k in range(1, R):
        await_recv("b", rows(rb, row_peer(k), blk), recv_b.at[row_peer(k)])
    total = rb[0:blk, :]
    for q in range(1, R):
        total = total + rb[q * blk:(q + 1) * blk, :]

    def stage_2():
        for k in range(1, n):
            src = a * n + b_peer(k)
            await_recv("v", rows(vg, src, vm), recv_v.at[0, src])
            for j in range(1, n):
                push("v", rows(vg, src, vm), rows(vg, src, vm), recv_v.at[0, src], (a_peer(j) * n + b, c))
        for k in range(1, n):
            src = a_peer(k) * n + b
            await_recv("v", rows(vcg, src, vm), recv_v.at[1, src])
            for j in range(1, n):
                push("v", rows(vcg, src, vm), rows(vcg, src, vm), recv_v.at[1, src], (a * n + b_peer(j), c))

    def left_cotangents():
        for k in range(1, Z):
            push("u", uc_ref, rows(ucg, c, um), recv_u.at[1, c], (r, 2 * z_peer(k) + h))

    mine = h * R + r
    if piece != blk:
        p2[...] = total
        for k in range(1, Z):
            push("c", rows(p2, z_peer(k), piece), rows(rc, z, piece), recv_c.at[z], (r, 2 * z_peer(k) + h))
        rows(rc, z, piece)[...] = rows(p2, z, piece)[...]
    else:
        rows(rc, z, blk)[...] = total
        for k in range(1, Z):
            push("c", rows(rc, z, blk), rows(rc, z, blk), recv_c.at[z], (r, 2 * z_peer(k) + h))
    for k in range(1, Z):
        await_recv("c", rows(rc, z_peer(k), piece), recv_c.at[z_peer(k)])
    total = rc[0:piece, :]
    for q in range(1, Z):
        total = total + rc[q * piece:(q + 1) * piece, :]
    at = mine * (blk // piece) + (z if piece != blk else 0)
    row_id = at * piece + lax.broadcasted_iota(jnp.int32, (piece, K), 0)
    diagonal = row_id == lax.broadcasted_iota(jnp.int32, (piece, K), 1)
    rows(core, at, piece)[...] = total + jnp.where(diagonal, sc_ref[...], 0.0)
    if piece != blk:
        for k in range(1, Z):
            push("f", rows(core, at, piece), rows(core, at, piece), recv_f.at[z], (r, 2 * z_peer(k) + h))
        left_cotangents()
        for k in range(1, Z):
            await_recv("f", rows(core, mine * Z + z_peer(k), piece), recv_f.at[z_peer(k)])
    else:
        left_cotangents()
    for k in range(1, R):
        push("d", rows(core, mine, blk), rows(core, mine, blk), recv_d.at[r], (row_peer(k), c))
    stage_2()
    push("e", rows(core, mine, blk), rows(core, mine, blk), recv_e.at[r], sib)

    for k in range(1, Z):
        src = 2 * z_peer(k) + h
        await_recv("u", rows(ug, src, um), recv_u.at[0, src])
        push("w", rows(ug, src, um), rows(ug, src, um), recv_u.at[0, src], sib)
    for k in range(1, R):
        q = row_peer(k)
        await_recv("d", rows(core, h * R + q, blk), recv_d.at[q])
        push("e", rows(core, h * R + q, blk), rows(core, h * R + q, blk), recv_e.at[q], sib)
    for k in range(Z):
        src = 2 * z_peer(k) + 1 - h
        await_recv("w", rows(ug, src, um), recv_u.at[0, src])
    uh[...], ul[...] = split(ug[...])
    xh[...], xl[...] = split(ug[...] * inv_row)
    for k in range(1, Z):
        src = 2 * z_peer(k) + h
        await_recv("u", rows(ucg, src, um), recv_u.at[1, src])
        push("w", rows(ucg, src, um), rows(ucg, src, um), recv_u.at[1, src], sib)
    width = 2 * LANES
    for q in range(R):
        await_recv("e", rows(core, (1 - h) * R + q, blk), recv_e.at[q])
    wh[...], wl[...] = split(core[...])
    for k in range(Z):
        src = 2 * z_peer(k) + 1 - h
        await_recv("w", rows(ucg, src, um), recv_u.at[1, src])

    @pl.loop(0, K // width)
    def _(i):
        here = pl.ds(pl.multiple_of(i * width, width), width)
        panel = dot3(uh[...], ul[...], wh[:, here], wl[:, here], NN)
        panel = panel + ucg[:, here] * (1.0 / s_ref[:, here])
        lh[:, here], ll[:, here] = split(panel)

    for k in range(1, n):
        await_recv("v", rows(vcg, a * n + b_peer(k), vm), recv_v.at[1, a * n + b_peer(k)])
        for j in range(1, n):
            src = a_peer(j) * n + b_peer(k)
            await_recv("v", rows(vcg, src, vm), recv_v.at[1, src])

    @pl.loop(0, out_ref.shape[1] // width)
    def _(i):
        here = pl.ds(pl.multiple_of(i * width, width), width)
        bh, bl = split(vcg[here, :])
        out_ref[:, here] = dot3(xh[...], xl[...], bh, bl, NT)

    for k in range(1, n):
        await_recv("v", rows(vg, a_peer(k) * n + b, vm), recv_v.at[0, a_peer(k) * n + b])
        for j in range(1, n):
            src = a_peer(k) * n + b_peer(j)
            await_recv("v", rows(vg, src, vm), recv_v.at[0, src])

    @pl.loop(0, out_ref.shape[1] // width)
    def _(i):
        here = pl.ds(pl.multiple_of(i * width, width), width)
        bh, bl = split(vg[here, :])
        out_ref[:, here] += dot3(lh[...], ll[...], bh, bl, NT)

    for copy in sends:
        copy.wait_send()


def local(R, C, left_factor, left_cotangent, right_factor, right_cotangent, singular, singular_cotangent):
    um, K = left_factor.shape
    vm = right_factor.shape[0]
    n, Z = math.isqrt(R), C // 2
    M, N = um * C, vm * R
    blk = K // 2 // R
    piece = blk // Z if blk % (8 * Z) == 0 else blk
    vmem = pl.BlockSpec(memory_space=pltpu.VMEM)
    dma = pltpu.SemaphoreType.DMA
    f32 = [
        (M, K), (M, K), (N, K), (N, K), (K, K), (K, K), (K, LANES), (K, K),
        (K // 2, K), (K // 2, K), (R * blk, K), (blk, K), (Z * piece, K), (K, K),
    ]
    b16 = [(K, K)] * 2 + [(M, K)] * 6
    scratch = [pltpu.VMEM(shape, F32) for shape in f32] + [pltpu.VMEM(shape, BF16) for shape in b16]
    scratch += [
        dma((4,)), dma((4 * (n - 1) + 2 * (n - 1) ** 2 + 4 * Z + 3 * R + 2 * Z,)),
        dma((2, R)), dma((2, C)), dma((1,)), dma((R,)), dma((Z,)), dma((R,)), dma((R,)), dma((Z,)),
    ]
    return pl.pallas_call(
        functools.partial(kernel, R, C),
        out_shape=jax.ShapeDtypeStruct((M, N), F32),
        in_specs=[pl.BlockSpec(memory_space=pltpu.HBM)] * 4 + [vmem] * 2,
        out_specs=vmem,
        scratch_shapes=scratch,
        compiler_params=pltpu.CompilerParams(
            collective_id=0, has_side_effects=True, vmem_limit_bytes=62 * 1024 * 1024
        ),
    )(
        left_factor, left_cotangent, right_factor, right_cotangent,
        singular.reshape(1, K), singular_cotangent.reshape(1, K),
    )


def solution(mesh):
    placed = (
        P(("row", "col"), None),
        P(("row", "col"), None),
        P(("col", "row"), None),
        P(("col", "row"), None),
        P(),
        P(),
    )
    return jax.shard_map(
        functools.partial(local, mesh.shape["row"], mesh.shape["col"]),
        mesh=mesh, in_specs=placed, out_specs=P("row", "col"), check_vma=False,
    )
```

```python
import functools
import math

import jax
import jax.numpy as jnp
from jax import lax
from jax.experimental import pallas as pl
from jax.experimental.pallas import tpu as pltpu
from jax.sharding import PartitionSpec as P

MESH = pl.DeviceIdType.MESH
F32 = jnp.float32
BF16 = jnp.bfloat16
LANES = 128
NT = (((1,), (1,)), ((), ()))
NN = (((1,), (0,)), ((), ()))
TN = (((0,), (0,)), ((), ()))


def split(x):
    hi = x.astype(BF16)
    return hi, (x - hi.astype(F32)).astype(BF16)


def dot3(ah, al, bh, bl, dims):
    dot = functools.partial(lax.dot_general, dimension_numbers=dims, preferred_element_type=F32)
    return dot(ah, bh) + (dot(ah, bl) + dot(al, bh))


def kernel(
    R, C,
    u_ref, uc_ref, v_ref, vc_ref, s_in, sc_in, out_ref,
    s_ref, sc_ref,
    ug, ucg, vg, vcg, gl, gr, scol, part, ra, p1, rb, p2, rc, core,
    wh, wl, uh, ul, lh, ll, xh, xl,
    load, send, recv_v, recv_u, recv_a, recv_b, recv_c, recv_d, recv_e, recv_f,
):
    n = math.isqrt(R)
    Z = C // 2
    r, c = lax.axis_index("row"), lax.axis_index("col")
    a, b = r // n, r % n
    z, h = c // 2, c % 2
    sib = (r, c + 1 - 2 * h)
    um, vm = u_ref.shape[0], v_ref.shape[0]
    K = u_ref.shape[1]
    half = K // 2
    blk = half // R
    piece = blk // Z if blk % (8 * Z) == 0 else blk

    def row_peer(k):
        return lax.rem(r + k, R)

    def z_peer(k):
        return lax.rem(z + k, Z)

    def a_peer(k):
        return lax.rem(a + k, n)

    def b_peer(k):
        return lax.rem(b + k, n)

    def rows(ref, index, size):
        return ref.at[pl.ds(pl.multiple_of(index * size, size), size)]

    loads = [
        pltpu.make_async_copy(src, dst, load.at[i])
        for i, (src, dst) in enumerate((
            (u_ref, rows(ug, c, um)), (uc_ref, rows(ucg, c, um)),
            (v_ref, rows(vg, r, vm)), (vc_ref, rows(vcg, r, vm)), (s_in, s_ref), (sc_in, sc_ref),
        ))
    ]
    barrier = pltpu.get_barrier_semaphore()
    pl.semaphore_signal(barrier, inc=1, device_id=sib, device_id_type=MESH)
    for k in range(1, R):
        pl.semaphore_signal(barrier, inc=1, device_id=(row_peer(k), c), device_id_type=MESH)
    for k in range(1, Z):
        pl.semaphore_signal(barrier, inc=1, device_id=(r, 2 * z_peer(k) + h), device_id_type=MESH)
    for copy in loads:
        copy.start()

    pl.semaphore_wait(barrier, 1 + (R - 1) + (Z - 1))

    sends = []

    def push(tag, src, dst, recv, to):
        copy = pltpu.make_async_remote_copy(
            src_ref=src, dst_ref=dst, send_sem=send.at[len(sends)], recv_sem=recv,
            device_id=to, device_id_type=MESH,
        )
        copy.start()
        sends.append(copy)

    def await_recv(tag, dst, recv):
        pltpu.make_async_remote_copy(
            src_ref=dst, dst_ref=dst, send_sem=send.at[0], recv_sem=recv,
            device_id=sib, device_id_type=MESH,
        ).wait_recv()


    for k in range(1, n):
        push("v", v_ref, rows(vg, r, vm), recv_v.at[0, r], (a * n + b_peer(k), c))
    for k in range(1, n):
        push("v", vc_ref, rows(vcg, r, vm), recv_v.at[1, r], (a_peer(k) * n + b, c))
    for k in range(1, Z):
        push("u", u_ref, rows(ug, c, um), recv_u.at[0, c], (r, 2 * z_peer(k) + h))

    highest = lax.Precision.HIGHEST
    for copy in loads:
        copy.wait()
    gl[...] = lax.dot_general(
        rows(ug, c, um)[...], rows(ucg, c, um)[...], TN, precision=highest, preferred_element_type=F32
    )
    gr[...] = lax.dot_general(
        rows(vg, r, vm)[...], rows(vcg, r, vm)[...], TN, precision=highest, preferred_element_type=F32
    )
    s_row = s_ref[...]
    inv_row = 1.0 / s_row
    scol[...] = jnp.broadcast_to(s_row, (LANES, K)).T

    @pl.loop(0, K // LANES)
    def _(i):
        here = pl.ds(pl.multiple_of(i * LANES, LANES), LANES)
        s_col = scol[here, 0:1]
        inv_col = 1.0 / s_col
        spread = s_row * s_row - s_col * s_col
        row_id = i * LANES + lax.broadcasted_iota(jnp.int32, (LANES, K), 0)
        diagonal = row_id == lax.broadcasted_iota(jnp.int32, (LANES, K), 1)
        divided = jnp.where(diagonal, 0.0, 1.0 / jnp.where(diagonal, 1.0, spread))
        left, left_t = gl[here, :], gl[:, here].T
        right, right_t = gr[here, :], gr[:, here].T
        value = divided * (left - left_t) * s_row + s_col * (divided * (right - right_t))
        part[here, :] = value - left * inv_row - inv_col * right_t

    push("a", rows(part, 1 - h, half), ra, recv_a.at[0], sib)
    await_recv("a", ra, recv_a.at[0])
    p1[...] = rows(part, h, half)[...] + ra[...]
    for k in range(1, R):
        push("b", rows(p1, row_peer(k), blk), rows(rb, r, blk), recv_b.at[r], (row_peer(k), c))
    rows(rb, r, blk)[...] = rows(p1, r, blk)[...]
    push("w", u_ref, rows(ug, c, um), recv_u.at[0, c], sib)
    push("w", uc_ref, rows(ucg, c, um), recv_u.at[1, c], sib)
    for k in range(1, R):
        await_recv("b", rows(rb, row_peer(k), blk), recv_b.at[row_peer(k)])
    total = rb[0:blk, :]
    for q in range(1, R):
        total = total + rb[q * blk:(q + 1) * blk, :]

    def stage_2():
        for k in range(1, n):
            src = a * n + b_peer(k)
            await_recv("v", rows(vg, src, vm), recv_v.at[0, src])
            for j in range(1, n):
                push("v", rows(vg, src, vm), rows(vg, src, vm), recv_v.at[0, src], (a_peer(j) * n + b, c))
        for k in range(1, n):
            src = a_peer(k) * n + b
            await_recv("v", rows(vcg, src, vm), recv_v.at[1, src])
            for j in range(1, n):
                push("v", rows(vcg, src, vm), rows(vcg, src, vm), recv_v.at[1, src], (a * n + b_peer(j), c))

    def left_cotangents():
        for k in range(1, Z):
            push("u", uc_ref, rows(ucg, c, um), recv_u.at[1, c], (r, 2 * z_peer(k) + h))

    mine = h * R + r
    if piece != blk:
        p2[...] = total
        for k in range(1, Z):
            push("c", rows(p2, z_peer(k), piece), rows(rc, z, piece), recv_c.at[z], (r, 2 * z_peer(k) + h))
        rows(rc, z, piece)[...] = rows(p2, z, piece)[...]
    else:
        rows(rc, z, blk)[...] = total
        for k in range(1, Z):
            push("c", rows(rc, z, blk), rows(rc, z, blk), recv_c.at[z], (r, 2 * z_peer(k) + h))
    for k in range(1, n):
        push("v", v_ref, rows(vg, r, vm), recv_v.at[0, r], (a_peer(k) * n + b, c))
    for k in range(1, n):
        push("v", vc_ref, rows(vcg, r, vm), recv_v.at[1, r], (a * n + b_peer(k), c))
    for k in range(1, Z):
        await_recv("c", rows(rc, z_peer(k), piece), recv_c.at[z_peer(k)])
    total = rc[0:piece, :]
    for q in range(1, Z):
        total = total + rc[q * piece:(q + 1) * piece, :]
    at = mine * (blk // piece) + (z if piece != blk else 0)
    row_id = at * piece + lax.broadcasted_iota(jnp.int32, (piece, K), 0)
    diagonal = row_id == lax.broadcasted_iota(jnp.int32, (piece, K), 1)
    rows(core, at, piece)[...] = total + jnp.where(diagonal, sc_ref[...], 0.0)
    if piece != blk:
        for k in range(1, Z):
            push("f", rows(core, at, piece), rows(core, at, piece), recv_f.at[z], (r, 2 * z_peer(k) + h))
        for k in range(1, Z):
            await_recv("f", rows(core, mine * Z + z_peer(k), piece), recv_f.at[z_peer(k)])
        left_cotangents()
    else:
        left_cotangents()
    for k in range(1, R):
        push("d", rows(core, mine, blk), rows(core, mine, blk), recv_d.at[r], (row_peer(k), c))
    stage_2()
    push("e", rows(core, mine, blk), rows(core, mine, blk), recv_e.at[r], sib)

    for k in range(1, Z):
        src = 2 * z_peer(k) + h
        await_recv("u", rows(ug, src, um), recv_u.at[0, src])
        push("w", rows(ug, src, um), rows(ug, src, um), recv_u.at[0, src], sib)
    for k in range(1, R):
        q = row_peer(k)
        await_recv("d", rows(core, h * R + q, blk), recv_d.at[q])
        push("e", rows(core, h * R + q, blk), rows(core, h * R + q, blk), recv_e.at[q], sib)
    for k in range(Z):
        src = 2 * z_peer(k) + 1 - h
        await_recv("w", rows(ug, src, um), recv_u.at[0, src])
    uh[...], ul[...] = split(ug[...])
    xh[...], xl[...] = split(ug[...] * inv_row)
    for k in range(1, Z):
        src = 2 * z_peer(k) + h
        await_recv("u", rows(ucg, src, um), recv_u.at[1, src])
        push("w", rows(ucg, src, um), rows(ucg, src, um), recv_u.at[1, src], sib)
    width = 2 * LANES
    for q in range(R):
        await_recv("e", rows(core, (1 - h) * R + q, blk), recv_e.at[q])
    wh[...], wl[...] = split(core[...])
    for k in range(Z):
        src = 2 * z_peer(k) + 1 - h
        await_recv("w", rows(ucg, src, um), recv_u.at[1, src])

    @pl.loop(0, K // width)
    def _(i):
        here = pl.ds(pl.multiple_of(i * width, width), width)
        panel = dot3(uh[...], ul[...], wh[:, here], wl[:, here], NN)
        panel = panel + ucg[:, here] * (1.0 / s_ref[:, here])
        lh[:, here], ll[:, here] = split(panel)

    def columns(q):
        at = slice(q * vm, (q + 1) * vm)
        bh, bl = split(vcg[at, :])
        ch, cl = split(vg[at, :])
        out_ref[:, at] = dot3(xh[...], xl[...], bh, bl, NT) + dot3(lh[...], ll[...], ch, cl, NT)

    for k in range(1, n):
        await_recv("v", rows(vcg, a * n + b_peer(k), vm), recv_v.at[1, a * n + b_peer(k)])
        await_recv("v", rows(vg, a_peer(k) * n + b, vm), recv_v.at[0, a_peer(k) * n + b])
    for q in range(R):
        pl.when((a == q // n) | (b == q % n))(functools.partial(columns, q))
    for k in range(1, n):
        for j in range(1, n):
            src = a_peer(k) * n + b_peer(j)
            await_recv("v", rows(vcg, src, vm), recv_v.at[1, src])
            await_recv("v", rows(vg, src, vm), recv_v.at[0, src])
    for q in range(R):
        pl.when((a != q // n) & (b != q % n))(functools.partial(columns, q))

    for copy in sends:
        copy.wait_send()


def local(R, C, left_factor, left_cotangent, right_factor, right_cotangent, singular, singular_cotangent):
    um, K = left_factor.shape
    vm = right_factor.shape[0]
    n, Z = math.isqrt(R), C // 2
    M, N = um * C, vm * R
    blk = K // 2 // R
    piece = blk // Z if blk % (8 * Z) == 0 else blk
    vmem = pl.BlockSpec(memory_space=pltpu.VMEM)
    dma = pltpu.SemaphoreType.DMA
    f32 = [
        (1, K), (1, K),
        (M, K), (M, K), (N, K), (N, K), (K, K), (K, K), (K, LANES), (K, K),
        (K // 2, K), (K // 2, K), (R * blk, K), (blk, K), (Z * piece, K), (K, K),
    ]
    b16 = [(K, K)] * 2 + [(M, K)] * 6
    scratch = [pltpu.VMEM(shape, F32) for shape in f32] + [pltpu.VMEM(shape, BF16) for shape in b16]
    scratch += [
        dma((6,)), dma((4 * (n - 1) + 2 * (n - 1) ** 2 + 4 * Z + 3 * R + 2 * Z,)),
        dma((2, R)), dma((2, C)), dma((1,)), dma((R,)), dma((Z,)), dma((R,)), dma((R,)), dma((Z,)),
    ]
    return pl.pallas_call(
        functools.partial(kernel, R, C),
        out_shape=jax.ShapeDtypeStruct((M, N), F32),
        in_specs=[pl.BlockSpec(memory_space=pltpu.HBM)] * 6,
        out_specs=vmem,
        scratch_shapes=scratch,
        compiler_params=pltpu.CompilerParams(
            collective_id=0, has_side_effects=True, vmem_limit_bytes=62 * 1024 * 1024
        ),
    )(
        left_factor, left_cotangent, right_factor, right_cotangent,
        singular.reshape(1, K), singular_cotangent.reshape(1, K),
    )


def solution(mesh):
    placed = (
        P(("row", "col"), None),
        P(("row", "col"), None),
        P(("col", "row"), None),
        P(("col", "row"), None),
        P(),
        P(),
    )
    return jax.shard_map(
        functools.partial(local, mesh.shape["row"], mesh.shape["col"]),
        mesh=mesh, in_specs=placed, out_specs=P("row", "col"), check_vma=False,
    )
```
